32 devices in a mesh: section: 2 (over x), ctx: 16 (over z, y, core).
Axes of the slice: x: 2, y: 2, z: 4, core: 2. Of those that a mesh axis runs over, the one named last changes fastest.
Arguments:
- resid: bfloat16 [2, 4096, 4096], P('section', 'ctx'), may hold values from -16 to 16
- queries: bfloat16 [2, 4096, 512], P('section', 'ctx'), may hold values from -8 to 8
- keyvals: bfloat16 [2, 4096, 256], P('section', 'ctx'), may hold values from -8 to 8
- run_max: float32 [2, 4096, 4], P('section', 'ctx'), may hold values from 1 to 4
- run_sum: float32 [2, 4096, 4], P('section', 'ctx'), may hold values from 128 to 1024
- run_out: float32 [2, 4096, 512], P('section', 'ctx'), may hold values from -384 to 384
- span_pair: int32 [16, 2], replicated, may hold values from 0 to 31, as said below
- norm_gain: float32 [2, 4096], P('section'), may hold values from 0.5 to 1.5
- w_query: bfloat16 [2, 4096, 512], P('section', 'ctx'), may hold values from -0.095458984 to 0.095458984
- w_keyval: bfloat16 [2, 4096, 256], P('section', 'ctx'), may hold values from -0.095458984 to 0.095458984
- w_out: bfloat16 [2, 512, 4096], P('section', None, 'ctx'), may hold values from -0.59765625 to 0.59765625
Outputs:
- queries_next: bfloat16 [2, 4096, 512], P('section', 'ctx')
- keyvals_next: bfloat16 [2, 4096, 256], P('section', 'ctx')
- max_next: float32 [2, 4096, 4], P('section', 'ctx')
- sum_next: float32 [2, 4096, 4], P('section', 'ctx')
- out_next: float32 [2, 4096, 512], P('section', 'ctx')
The draws below stay inside these ranges and needn't reach their ends.
Inputs may be any that keep to these rules, and one draw needn't show every extreme that they name: `span_pair`: each ctx index holds blocks c and 31 - c, its first column running once over 0 to 15.
All inputs are finite; a program needn't handle non-finite values.
Results may differ from the reference program's by a relative error of at most 0.005.
The reference program's roundings to bfloat16 on the way (of `attended`, `finished`, `incoming` and `normed`) count: a program that leaves them out, or rounds other values in their place, can miss the bound.
Values may be sent and summed in bfloat16 or wider, within the bound.
A program may use at most 64 MiB of HBM per device.

```python
import math
import jax
import jax.numpy as jnp
from jax import lax

D = 4096
HEAD = 128
QHEADS = 4
TOK_DEV = 256
SPAN = 128
SEQ = 4096
SECTIONS = 2


def sign_vector(key, length):
    bits = jax.random.randint(key, (length,), 0, 2)
    return jnp.where(bits == 0, -1.0, 1.0).astype(jnp.float32)


def base_noise(key, shape):
    values = jnp.clip(jax.random.normal(key, shape, jnp.float32), -6.0, 6.0)
    return values


def row_levels(key, shape, lower, upper):
    chosen = jax.random.randint(jax.random.fold_in(key, 1), shape, 0, 16) == 0
    strength = jax.random.uniform(jax.random.fold_in(key, 2), shape, jnp.float32, lower, upper)
    return jnp.where(chosen, strength, 0.0).astype(jnp.float32)


def draw_span_pair(key, part):
    cycle_size = SEQ // TOK_DEV
    shuffled = jax.random.permutation(key, cycle_size).astype(jnp.int32)
    return jnp.stack([shuffled, 2 * cycle_size - 1 - shuffled], axis=-1).astype(jnp.int32)


def draw_resid(key, part):
    sigma = sign_vector(jax.random.fold_in(key, 11), D)

    def one_section(section):
        local = jax.random.fold_in(jax.random.fold_in(key, 21), section)
        noise = base_noise(jax.random.fold_in(local, 3), (SEQ, D))
        level = row_levels(local, (SEQ, 1), 5.0, 8.0)
        return (noise + level * sigma[None, :]).astype(jnp.bfloat16)
    return lax.map(one_section, jnp.arange(SECTIONS, dtype=jnp.int32))


def draw_w_query(key, part):
    sigma = sign_vector(jax.random.fold_in(key, 11), D)
    tau = sign_vector(jax.random.fold_in(key, 12), HEAD)
    local = jax.random.fold_in(key, 31)
    noise = base_noise(jax.random.fold_in(local, 1), (SECTIONS, D, QHEADS, HEAD)) * D ** (-0.5)
    head_level = jax.random.uniform(jax.random.fold_in(local, 2), (SECTIONS, 1, QHEADS, 1), jnp.float32, 4.0, 6.5)
    aligned = head_level * sigma[None, :, None, None] * tau[None, None, None, :] * (1.0 / D)
    return (noise + aligned).reshape(SECTIONS, D, QHEADS * HEAD).astype(jnp.bfloat16)


def draw_w_keyval(key, part):
    sigma = sign_vector(jax.random.fold_in(key, 11), D)
    tau = sign_vector(jax.random.fold_in(key, 12), HEAD)
    local = jax.random.fold_in(key, 41)
    noise = base_noise(jax.random.fold_in(local, 1), (SECTIONS, D, 2 * HEAD)) * D ** (-0.5)
    key_level = jax.random.uniform(jax.random.fold_in(local, 2), (SECTIONS, 1, 1), jnp.float32, 4.5, 6.0)
    aligned = key_level * sigma[None, :, None] * tau[None, None, :] * (1.0 / D)
    aligned = jnp.concatenate([aligned, jnp.zeros((SECTIONS, D, HEAD), jnp.float32)], axis=-1)
    return (noise + aligned).astype(jnp.bfloat16)


def draw_queries(key, part):
    tau = sign_vector(jax.random.fold_in(key, 13), HEAD)
    local = jax.random.fold_in(key, 51)
    noise = base_noise(jax.random.fold_in(local, 3), (SECTIONS, SEQ, QHEADS, HEAD))
    level = row_levels(local, (SECTIONS, SEQ, 1, 1), 3.5, 6.0)
    values = jnp.where(level > 0.0, level * tau[None, None, None, :] + 0.3 * noise, noise)
    return values.reshape(SECTIONS, SEQ, QHEADS * HEAD).astype(jnp.bfloat16)


def draw_keyvals(key, part):
    tau = sign_vector(jax.random.fold_in(key, 13), HEAD)
    local = jax.random.fold_in(key, 61)
    key_noise = base_noise(jax.random.fold_in(local, 3), (SECTIONS, SEQ, HEAD))
    value_noise = base_noise(jax.random.fold_in(local, 4), (SECTIONS, SEQ, HEAD))
    level = row_levels(local, (SECTIONS, SEQ, 1), 4.0, 6.0)
    key_part = jnp.where(level > 0.0, level * tau[None, None, :] + 0.3 * key_noise, key_noise)
    return jnp.concatenate([key_part, value_noise], axis=-1).astype(jnp.bfloat16)


def shard_levels(key, shape, shards, low, high):
    loudness = 1.0
    for position, shards_of in shards:
        steps = jax.random.uniform(jax.random.fold_in(jax.random.fold_in(key, 6), position), (shards_of,), jnp.float32, low / len(shards), high / len(shards))
        loudness = loudness * jnp.repeat(jnp.exp(steps), shape[position] // shards_of).reshape((-1,) + (1,) * (len(shape) - 1 - position))
    return loudness


def gaussian(rng, shape, width, reach, pieces=(), kind=jnp.bfloat16):
    factor_of = shard_levels(rng, shape, pieces, -0.22, 0.18) if pieces else 1.0
    result = jax.random.normal(rng, shape, jnp.float32) * width * factor_of
    return jnp.minimum(jnp.maximum(result, -reach), reach).astype(kind)


def setup_inputs(seed: int = 0) -> dict:
    streams_of = jax.random.split(jax.random.key(seed), 12)
    resid = draw_resid(jax.random.fold_in(streams_of[11], 71), 0)
    queries = draw_queries(jax.random.fold_in(streams_of[11], 71), 0)
    keyvals = draw_keyvals(jax.random.fold_in(streams_of[11], 71), 0)
    run_max = jnp.clip(1.0 + 3.0 * jax.random.uniform(streams_of[3], (SECTIONS, SEQ, QHEADS), jnp.float32) ** shard_levels(streams_of[3], (SECTIONS, SEQ, QHEADS), ((0, 2), (1, 16)), -0.2, 0.2), 1.0, 4.0)
    run_sum = jnp.clip(jnp.exp(math.log(1024.0) - 2.0794415 * jax.random.uniform(streams_of[4], (SECTIONS, SEQ, QHEADS), jnp.float32) ** shard_levels(streams_of[4], (SECTIONS, SEQ, QHEADS), ((0, 2), (1, 16)), -0.2, 0.2)), 128.0, 1024.0)
    run_out = gaussian(streams_of[5], (SECTIONS, SEQ, QHEADS * HEAD), (SPAN // 2), 384.0, ((0, 2), (1, 16)), jnp.float32)
    span_pair = draw_span_pair(jax.random.fold_in(streams_of[11], 71), 0)
    norm_gain = jnp.clip(1.0 + 0.1 * jax.random.normal(streams_of[7], (SECTIONS, D), jnp.float32), 0.5, 1.5)
    w_query = draw_w_query(jax.random.fold_in(streams_of[11], 71), 0)
    w_keyval = draw_w_keyval(jax.random.fold_in(streams_of[11], 71), 0)
    w_out = gaussian(streams_of[10], (SECTIONS, QHEADS * HEAD, D), 0.1, 0.59765625, ((0, 2), (2, 16)))
    return dict(resid=resid, queries=queries, keyvals=keyvals, run_max=run_max, run_sum=run_sum, run_out=run_out, span_pair=span_pair, norm_gain=norm_gain, w_query=w_query, w_keyval=w_keyval, w_out=w_out)


def positions(span_pair, rows_here):
    half_rows = rows_here // 2
    offsets = jnp.arange(rows_here, dtype=jnp.int32)
    span_index = span_pair[:, offsets // half_rows]
    return (span_index * half_rows + offsets % half_rows).astype(jnp.int32)

def flash_step(query_rows, key_block, pos_query, pos_key, old_max, old_sum, old_out):
    rows_here = query_rows.shape[0]
    query_heads = query_rows.reshape(rows_here, QHEADS, HEAD).astype(jnp.float32)
    key_part = key_block[:, :HEAD].astype(jnp.float32)
    value_part = key_block[:, HEAD:].astype(jnp.float32)
    scores = jnp.einsum('qhd,kd->hqk', query_heads, key_part) * HEAD ** (-0.5)
    keep = pos_key[None, None, :] <= pos_query[None, :, None]
    masked = jnp.where(keep, scores, -1e+30)
    prior_max = old_max.T
    new_max = jnp.maximum(prior_max, lax.optimization_barrier(jnp.max(masked, axis=-1)))
    exp_scores = jnp.where(keep, jnp.exp(scores - new_max[:, :, None]), 0.0)
    decay_factor = jnp.exp(prior_max - new_max)
    new_sum = old_sum.T * decay_factor + lax.optimization_barrier(jnp.sum(exp_scores, axis=-1))
    rounded = exp_scores.astype(jnp.bfloat16).astype(jnp.float32)
    contrib = jnp.einsum('hqk,kd->qhd', rounded, value_part)
    new_out = old_out.reshape(rows_here, QHEADS, HEAD) * decay_factor.T[:, :, None] + contrib
    return (new_max.T, new_sum.T, new_out.reshape(rows_here, QHEADS * HEAD))

def reference(resid, queries, keyvals, run_max, run_sum, run_out, span_pair, norm_gain, w_query, w_keyval, w_out):
    cycle_size = span_pair.shape[0]
    sections = resid.shape[0]
    rows_here = resid.shape[1] // cycle_size
    pos_all = positions(span_pair, rows_here)
    pos_near = jnp.roll(pos_all, -1, axis=0)
    pos_far = jnp.roll(pos_all, -2, axis=0)
    finished = []
    for section_index in range(sections):
        query_dev = queries[section_index].reshape(cycle_size, rows_here, -1)
        keyval_dev = keyvals[section_index].reshape(cycle_size, rows_here, -1)
        near_block = jnp.roll(keyval_dev, -1, axis=0)
        far_block = jnp.roll(keyval_dev, -2, axis=0)
        max_dev = run_max[section_index].reshape(cycle_size, rows_here, -1)
        sum_dev = run_sum[section_index].reshape(cycle_size, rows_here, -1)
        out_dev = run_out[section_index].reshape(cycle_size, rows_here, -1)

        def per_device(inputs_one):
            query_one, far_one, near_one, pos_q, pos_f, pos_n, max_one, sum_one, out_one = inputs_one
            max_one, sum_one, out_one = flash_step(query_one, far_one, pos_q, pos_f, max_one, sum_one, out_one)
            max_one, sum_one, out_one = flash_step(query_one, near_one, pos_q, pos_n, max_one, sum_one, out_one)
            divided = out_one.reshape(rows_here, QHEADS, HEAD) / sum_one[:, :, None]
            return divided.reshape(rows_here, QHEADS * HEAD).astype(jnp.bfloat16)
        attended = lax.map(per_device, (query_dev, far_block, near_block, pos_all, pos_far, pos_near, max_dev, sum_dev, out_dev))
        attended = attended.reshape(cycle_size * rows_here, -1)
        projected = jnp.dot(attended, w_out[section_index], preferred_element_type=jnp.float32)
        finished.append((resid[section_index].astype(jnp.float32) + projected).astype(jnp.bfloat16))
    outs_query, outs_keyval, outs_max, outs_sum, outs_out = ([], [], [], [], [])
    for section_index in range(sections):
        incoming = finished[(section_index - 1) % sections]
        wide = incoming.astype(jnp.float32)
        mean_square = lax.optimization_barrier(jnp.mean(wide * wide, axis=-1, keepdims=True))
        normed = (wide * lax.rsqrt(mean_square + 1e-05) * norm_gain[section_index][None, :]).astype(jnp.bfloat16)
        query_new = jnp.dot(normed, w_query[section_index], preferred_element_type=jnp.float32).astype(jnp.bfloat16)
        keyval_new = jnp.dot(normed, w_keyval[section_index], preferred_element_type=jnp.float32).astype(jnp.bfloat16)
        query_dev = query_new.reshape(cycle_size, rows_here, -1)
        keyval_dev = keyval_new.reshape(cycle_size, rows_here, -1)

        def first_step(inputs_one):
            query_one, keyval_one, pos_q = inputs_one
            start_max = jnp.full((rows_here, QHEADS), -1e+30, jnp.float32)
            start_sum = jnp.zeros((rows_here, QHEADS), jnp.float32)
            start_out = jnp.zeros((rows_here, QHEADS * HEAD), jnp.float32)
            return flash_step(query_one, keyval_one, pos_q, pos_q, start_max, start_sum, start_out)
        max_new, sum_new, out_new = lax.map(first_step, (query_dev, keyval_dev, pos_all))
        outs_query.append(query_new)
        outs_keyval.append(keyval_new)
        outs_max.append(max_new.reshape(cycle_size * rows_here, -1))
        outs_sum.append(sum_new.reshape(cycle_size * rows_here, -1))
        outs_out.append(out_new.reshape(cycle_size * rows_here, -1))
    return (jnp.stack(outs_query), jnp.stack(outs_keyval), jnp.stack(outs_max), jnp.stack(outs_sum), jnp.stack(outs_out))
```

```python
import functools

import jax
import jax.numpy as jnp
from jax import lax
from jax.experimental import pallas as pl
from jax.experimental.pallas import tpu as pltpu
from jax.sharding import PartitionSpec as P

HEAD = 128
QHEADS = 4
MESH = pl.DeviceIdType.MESH
CORE, ACROSS, UP, DOWN = range(4)
OUT, KV, QA, QB = range(4)


def kernel(
    sections,
    n,
    resid_hbm,
    queries_ref,
    keyvals_hbm,
    max_ref,
    sum_ref,
    run_ref,
    span_ref,
    gain_hbm,
    wq_hbm,
    wkv_hbm,
    wo_hbm,
    q_out,
    kv_out,
    max_out,
    sum_out,
    out_out,
    wo_buf,
    w_buf,
    resid_buf,
    fin_buf,
    gain_buf,
    near_buf,
    att_buf,
    acc_buf,
    sq_buf,
    ship_buf,
    in_buf,
    local_sem,
    send_sem,
    recv_sem,
    nsend_sem,
    nrecv_sem,
    xsend_sem,
    gain_sem,
    rsend_sem,
    rrecv_sem,
):
    sec = lax.axis_index("section")
    me = lax.axis_index("ctx")
    layers = n // 4
    z, y, c = me // 4, (me // 2) % 2, me % 2
    ahead = lax.rem(sec + 1, sections)
    behind = lax.rem(sec + sections - 1, sections)
    rows = resid_buf.shape[0]
    half = rows // 2
    unit = w_buf.shape[-1]

    load_resid = pltpu.make_async_copy(resid_hbm.at[0], resid_buf, local_sem.at[0])
    load_out = pltpu.make_async_copy(wo_hbm.at[0], wo_buf.at[me], local_sem.at[1])
    load_out.start()
    load_resid.start()

    def index(zz, yy, cc):
        return zz * 4 + yy * 2 + cc

    barrier = pltpu.get_barrier_semaphore()
    fixed = [
        (sec, index(z, y, 1 - c)),
        (sec, index(z, 1 - y, c)),
        (sec, lax.rem(me + 1, n)),
        (sec, lax.rem(me + 2, n)),
        (sec, lax.rem(me + n - 1, n)),
        (sec, lax.rem(me + n - 2, n)),
        (ahead, me),
        (behind, me),
    ]
    for peer in fixed:
        pl.semaphore_signal(barrier, inc=1, device_id=peer, device_id_type=MESH)

    @pl.when(z > 0)
    def _():
        pl.semaphore_signal(barrier, inc=1, device_id=(sec, me - 4), device_id_type=MESH)

    @pl.when(z < layers - 1)
    def _():
        pl.semaphore_signal(barrier, inc=1, device_id=(sec, me + 4), device_id_type=MESH)

    ends = jnp.where(z > 0, 1, 0) + jnp.where(z < layers - 1, 1, 0)
    pl.semaphore_wait(barrier, len(fixed) + ends)

    def remote(src, dst, send, recv, device):
        return pltpu.make_async_remote_copy(
            src_ref=src, dst_ref=dst, send_sem=send, recv_sem=recv,
            device_id=device, device_id_type=MESH,
        )

    near_copy = remote(keyvals_hbm.at[0], near_buf.at[0], nsend_sem.at[0], nrecv_sem.at[0],
                       (sec, lax.rem(me + n - 1, n)))
    far_copy = remote(keyvals_hbm.at[0], near_buf.at[1], nsend_sem.at[1], nrecv_sem.at[1],
                      (sec, lax.rem(me + n - 2, n)))
    near_copy.start()
    far_copy.start()

    def slot(u, src):
        return wo_buf.at[src] if u == OUT else w_buf.at[u - 1, src]

    swaps = []
    for u, ref in ((KV, wkv_hbm.at[0]), (QA, wq_hbm.at[0, :, 0:unit]),
                   (QB, wq_hbm.at[0, :, unit:2 * unit])):
        swaps.append(remote(ref, slot(u, me), xsend_sem.at[u], recv_sem.at[u, me], (behind, me)))
    gain_copy = remote(gain_hbm, gain_buf, xsend_sem.at[0], gain_sem.at[0], (behind, me))
    swaps[0].start()
    gain_copy.start()

    def hop(u, src, way):
        target = {
            CORE: index(z, y, 1 - c), ACROSS: index(z, 1 - y, c), UP: me + 4, DOWN: me - 4,
        }[way]
        return remote(slot(u, src), slot(u, src), send_sem.at[way, u, src],
                      recv_sem.at[u, src], (sec, target))

    def arrive(u, src):
        hop(u, src, CORE).wait_recv()

    def each_hop(u, d, other, act, arrived=None):
        yy = 1 - y if other else y

        def go(src, ways):
            if arrived is not None:
                arrived(src)
            for way in ways:
                if way == UP:
                    @pl.when(z < layers - 1)
                    def _():
                        act(hop(u, src, UP))
                elif way == DOWN:
                    @pl.when(z > 0)
                    def _():
                        act(hop(u, src, DOWN))
                else:
                    act(hop(u, src, way))

        onward = u == KV or not other
        across = [ACROSS] if (not other and (u != KV or d == 0)) else []
        if d == 0:
            go(index(z, yy, c), ([UP, DOWN] if onward else []) + across + [CORE])
        else:
            @pl.when(z >= d)
            def _():
                go(index(z - d, yy, c), ([UP] if onward else []) + across + [CORE])

            @pl.when(z + d < layers)
            def _():
                go(index(z + d, yy, c), ([DOWN] if onward else []) + across + [CORE])

    def event(u, d, other):
        own = u == OUT and d == 0 and not other
        each_hop(u, d, other, lambda copy: copy.start(),
                 None if own else lambda src: arrive(u, src))

    load_out.wait()
    event(OUT, 0, False)
    swaps[1].start()
    swaps[2].start()

    row = lax.broadcasted_iota(jnp.int32, (rows, 1), 0)
    col = lax.broadcasted_iota(jnp.int32, (1, rows), 1)

    def position(device, offsets):
        first, second = span_ref[device, 0], span_ref[device, 1]
        return jnp.where(offsets < half, first * half + offsets, second * half + offsets - half)

    pos_mine = position(me, row)

    def update(query, key, value, keep, m, l, acc):
        scores = lax.dot_general(
            query, key, (((1,), (1,)), ((), ())), preferred_element_type=jnp.float32
        ) * HEAD ** (-0.5)
        masked = jnp.where(keep, scores, -1e30)
        top = jnp.max(masked, axis=1, keepdims=True)
        m_new = top if m is None else jnp.maximum(m, top)
        p = jnp.where(keep, jnp.exp(scores - m_new), 0.0)
        l_new = jnp.sum(p, axis=1, keepdims=True)
        out = jnp.dot(p.astype(jnp.bfloat16), value, preferred_element_type=jnp.float32)
        if m is not None:
            decay = jnp.exp(m - m_new)
            l_new = l * decay + l_new
            out = acc * decay + out
        return m_new, l_new, out

    far_copy.wait_recv()
    near_copy.wait_recv()
    keep_far = position(lax.rem(me + 2, n), col) <= pos_mine
    keep_near = position(lax.rem(me + 1, n), col) <= pos_mine

    def attend(h):
        cols = slice(h * HEAD, (h + 1) * HEAD)
        query = queries_ref[0, :, cols]
        m, l, acc = max_ref[0, :, h:h + 1], sum_ref[0, :, h:h + 1], run_ref[0, :, cols]
        m, l, acc = update(query, near_buf[1, :, :HEAD], near_buf[1, :, HEAD:], keep_far, m, l, acc)
        m, l, acc = update(query, near_buf[0, :, :HEAD], near_buf[0, :, HEAD:], keep_near, m, l, acc)
        att_buf[:, cols] = (acc / l).astype(jnp.bfloat16)

    for h in range(QHEADS):
        attend(h)

    event(KV, 0, False)
    event(OUT, 1, False)
    event(OUT, 0, True)
    event(KV, 0, True)
    load_resid.wait()
    event(OUT, 2, False)
    event(OUT, 1, True)
    event(OUT, 3, False)
    event(QA, 0, False)
    event(KV, 1, False)
    event(OUT, 2, True)
    event(KV, 1, True)
    event(OUT, 3, True)

    sq_buf[...] = jnp.zeros_like(sq_buf)

    def project(step, carry):
        src = lax.rem(me + step, n)

        @pl.when(src % 2 != c)
        def _():
            arrive(OUT, src)

        at = pl.ds(pl.multiple_of(src * unit, unit), unit)
        block = jnp.dot(att_buf[...], wo_buf[src], preferred_element_type=jnp.float32)
        block = (resid_buf[:, at].astype(jnp.float32) + block).astype(jnp.bfloat16)
        fin_buf[src] = block
        wide = block.astype(jnp.float32)
        sq_buf[...] += wide * wide
        return carry

    lax.fori_loop(0, n, project, 0)
    gain_copy.wait_recv()
    mean_square = jnp.sum(sq_buf[...], axis=1, keepdims=True) * (1.0 / (n * unit))
    inverse = lax.rsqrt(mean_square + 1e-05)

    def normalise(src, carry):
        at = pl.ds(pl.multiple_of(src * unit, unit), unit)
        wide = fin_buf[src].astype(jnp.float32)
        fin_buf[src] = (wide * inverse * gain_buf[:, at]).astype(jnp.bfloat16)
        return carry

    event(KV, 2, False)
    event(KV, 2, True)
    event(QA, 1, False)
    event(QB, 0, False)
    lax.fori_loop(0, n, normalise, 0)
    event(KV, 3, False)
    event(KV, 3, True)
    event(QA, 0, True)
    event(QA, 2, False)
    event(QA, 1, True)

    def finish(u):
        acc_buf[...] = jnp.zeros_like(acc_buf)

        def add(src, carry):
            @pl.when(src % 2 != c)
            def _():
                arrive(u, src)

            acc_buf[...] += jnp.dot(fin_buf[src], w_buf[u - 1, src], preferred_element_type=jnp.float32)
            return carry

        lax.fori_loop(0, n, add, 0)
        ship_buf[u - 1] = acc_buf[...].astype(jnp.bfloat16)
        copy = remote(ship_buf.at[u - 1], in_buf.at[u - 1], rsend_sem.at[u - 1],
                      rrecv_sem.at[u - 1], (ahead, me))
        copy.start()
        return copy

    results = [finish(KV)]
    event(QA, 3, False)
    event(QB, 1, False)
    event(QA, 2, True)
    event(QB, 0, True)
    event(QB, 2, False)
    event(QA, 3, True)
    event(QB, 1, True)
    event(QB, 3, False)
    results.append(finish(QA))
    event(QB, 2, True)
    event(QB, 3, True)
    results.append(finish(QB))

    keep_own = position(me, col) <= pos_mine

    def own(h):
        query = in_buf[1 + h // 2, :, (h % 2) * HEAD:(h % 2 + 1) * HEAD]
        m, l, acc = update(query, in_buf[0, :, :HEAD], in_buf[0, :, HEAD:], keep_own, None, None, None)
        max_out[0, :, h:h + 1] = m
        sum_out[0, :, h:h + 1] = l
        out_out[0, :, h * HEAD:(h + 1) * HEAD] = acc

    results[0].wait_recv()
    kv_out[0] = in_buf[0]
    for pair in range(2):
        results[1 + pair].wait_recv()
        q_out[0, :, pair * unit:(pair + 1) * unit] = in_buf[1 + pair]
        own(2 * pair)
        own(2 * pair + 1)

    near_copy.wait_send()
    far_copy.wait_send()
    gain_copy.wait_send()
    for copy in swaps + results:
        copy.wait_send()
    for u in (OUT, KV, QA, QB):
        for d in range(layers):
            for other in (False, True):
                each_hop(u, d, other, lambda copy: copy.wait_send())


def fused(mesh, *args):
    sections, n = mesh.shape["section"], mesh.shape["ctx"]
    resid, queries, keyvals, run_max, run_sum, run_out = args[:6]
    rows, width = resid.shape[1:]
    unit = keyvals.shape[2]
    bf16, f32 = jnp.bfloat16, jnp.float32
    vmem = pl.BlockSpec(memory_space=pltpu.VMEM)
    smem = pl.BlockSpec(memory_space=pltpu.SMEM)
    hbm = pl.BlockSpec(memory_space=pl.ANY)
    dma = pltpu.SemaphoreType.DMA
    return pl.pallas_call(
        functools.partial(kernel, sections, n),
        out_shape=(
            jax.ShapeDtypeStruct(queries.shape, bf16),
            jax.ShapeDtypeStruct(keyvals.shape, bf16),
            jax.ShapeDtypeStruct(run_max.shape, f32),
            jax.ShapeDtypeStruct(run_sum.shape, f32),
            jax.ShapeDtypeStruct(run_out.shape, f32),
        ),
        in_specs=[hbm, vmem, hbm, vmem, vmem, vmem, smem, hbm, hbm, hbm, hbm],
        out_specs=[vmem] * 5,
        scratch_shapes=[
            pltpu.VMEM((n, 2 * unit, unit), bf16),
            pltpu.VMEM((3, n, unit, unit), bf16),
            pltpu.VMEM((rows, width), bf16),
            pltpu.VMEM((n, rows, unit), bf16),
            pltpu.VMEM((1, width), f32),
            pltpu.VMEM((2, rows, unit), bf16),
            pltpu.VMEM((rows, 2 * unit), bf16),
            pltpu.VMEM((rows, unit), f32),
            pltpu.VMEM((rows, unit), f32),
            pltpu.VMEM((3, rows, unit), bf16),
            pltpu.VMEM((3, rows, unit), bf16),
            dma((2,)),
            dma((4, 4, n)),
            dma((4, n)),
            dma((2,)),
            dma((2,)),
            dma((4,)),
            dma((1,)),
            dma((3,)),
            dma((3,)),
        ],
        compiler_params=pltpu.CompilerParams(
            collective_id=0, has_side_effects=True, vmem_limit_bytes=48 * 1024 * 1024
        ),
    )(*args)


def passed_along(value, axis, steps):
    count = lax.axis_size(axis)
    pairs = [(source, (source + steps) % count) for source in range(count)]
    return lax.ppermute(value, axis, pairs)


def device_positions(span_pair, device, rows_here):
    half_rows = rows_here // 2
    span_row = lax.dynamic_slice_in_dim(span_pair, device, 1, 0)[0]
    offsets = jnp.arange(rows_here, dtype=jnp.int32)
    span_index = jnp.where(offsets < half_rows, span_row[0], span_row[1])
    return span_index * half_rows + offsets % half_rows


def flash_step(query_rows, key_block, pos_query, pos_key, old_max, old_sum, old_out):
    rows_here = query_rows.shape[0]
    query_heads = query_rows.reshape(rows_here, QHEADS, HEAD)
    key_part = key_block[:, :HEAD]
    value_part = key_block[:, HEAD:]
    scores = jnp.einsum(
        "qhd,kd->hqk", query_heads, key_part, preferred_element_type=jnp.float32
    ) * HEAD ** (-0.5)
    keep = pos_key[None, None, :] <= pos_query[None, :, None]
    masked = jnp.where(keep, scores, -1e30)
    prior_max = old_max.T
    new_max = jnp.maximum(prior_max, jnp.max(masked, axis=-1))
    exp_scores = jnp.where(keep, jnp.exp(scores - new_max[:, :, None]), 0.0)
    decay_factor = jnp.exp(prior_max - new_max)
    new_sum = old_sum.T * decay_factor + jnp.sum(exp_scores, axis=-1)
    rounded = exp_scores.astype(jnp.bfloat16)
    contrib = jnp.einsum("hqk,kd->qhd", rounded, value_part, preferred_element_type=jnp.float32)
    new_out = old_out.reshape(rows_here, QHEADS, HEAD) * decay_factor.T[:, :, None] + contrib
    return (new_max.T, new_sum.T, new_out.reshape(rows_here, QHEADS * HEAD))


def add_rows(normed, shard_rows):
    return jnp.dot(normed, shard_rows, preferred_element_type=jnp.float32)


def per_device(
    resid,
    queries,
    keyvals,
    run_max,
    run_sum,
    run_out,
    span_pair,
    norm_gain,
    w_query,
    w_keyval,
    w_out,
):
    cycle_size = lax.axis_size("ctx")
    my_index = lax.axis_index("ctx")
    rows_here = resid.shape[1]
    pos_mine = device_positions(span_pair, my_index, rows_here)
    pos_near = device_positions(span_pair, (my_index + 1) % cycle_size, rows_here)
    pos_far = device_positions(span_pair, (my_index + 2) % cycle_size, rows_here)
    keyval_own = keyvals[0]
    near_block = passed_along(keyval_own, "ctx", -1)
    far_block = passed_along(near_block, "ctx", -1)
    max_now, sum_now, out_now = flash_step(
        queries[0], far_block, pos_mine, pos_far, run_max[0], run_sum[0], run_out[0]
    )
    max_now, sum_now, out_now = flash_step(
        queries[0], near_block, pos_mine, pos_near, max_now, sum_now, out_now
    )
    divided = out_now.reshape(rows_here, QHEADS, HEAD) / sum_now[:, :, None]
    attended = divided.reshape(rows_here, QHEADS * HEAD).astype(jnp.bfloat16)
    projected = jnp.dot(
        attended,
        lax.all_gather(w_out[0], "ctx", axis=1, tiled=True),
        preferred_element_type=jnp.float32,
    )
    finished = (resid[0].astype(jnp.float32) + projected).astype(jnp.bfloat16)
    incoming = passed_along(finished, "section", 1)
    wide = incoming.astype(jnp.float32)
    mean_square = jnp.mean(wide * wide, axis=-1, keepdims=True)
    normed = (wide * lax.rsqrt(mean_square + 1e-05) * norm_gain[0][None, :]).astype(jnp.bfloat16)

    def add_one(shard_rows):
        return add_rows(normed, shard_rows)

    query_sum = add_one(lax.all_gather(w_query[0], "ctx", axis=0, tiled=True))
    keyval_sum = add_one(lax.all_gather(w_keyval[0], "ctx", axis=0, tiled=True))
    query_new = query_sum.astype(jnp.bfloat16)
    keyval_new = keyval_sum.astype(jnp.bfloat16)
    start_max = jnp.full((rows_here, QHEADS), -1e30, jnp.float32)
    start_sum = jnp.zeros((rows_here, QHEADS), jnp.float32)
    start_out = jnp.zeros((rows_here, QHEADS * HEAD), jnp.float32)
    max_new, sum_new, out_new = flash_step(
        query_new, keyval_new, pos_mine, pos_mine, start_max, start_sum, start_out
    )
    return (query_new[None], keyval_new[None], max_new[None], sum_new[None], out_new[None])


def solution(mesh):
    placed = (
        P("section", "ctx", None),
        P("section", "ctx", None),
        P("section", "ctx", None),
        P("section", "ctx", None),
        P("section", "ctx", None),
        P("section", "ctx", None),
        P(),
        P("section", None),
        P("section", "ctx", None),
        P("section", "ctx", None),
        P("section", None, "ctx"),
    )
    def local(*args):
        rows, width = args[0].shape[1:]
        unit = args[2].shape[2]
        n = mesh.shape["ctx"]
        even = n % 4 == 0 and n <= 16 and mesh.shape["section"] > 1
        if even and rows == unit == 2 * HEAD and width == n * unit and rows % 32 == 0:
            return fused(mesh, *args)
        return per_device(*args)

    return jax.shard_map(
        local,
        mesh=mesh,
        in_specs=placed,
        out_specs=(
            P("section", "ctx", None),
            P("section", "ctx", None),
            P("section", "ctx", None),
            P("section", "ctx", None),
            P("section", "ctx", None),
        ),
        check_vma=False,
    )
```

```python
import functools

import jax
import jax.numpy as jnp
from jax import lax
from jax.experimental import pallas as pl
from jax.experimental.pallas import tpu as pltpu
from jax.sharding import PartitionSpec as P

HEAD = 128
QHEADS = 4
MESH = pl.DeviceIdType.MESH
CORE, ACROSS, UP, DOWN = range(4)
OUT, KV, QA, QB = range(4)
ACROSS_FIRST = QB
ATTEND, PROJECT, NORMALISE, FINISH = range(10, 14)

ORDER = [(OUT,0,0),(QB,0,0),(KV,0,0),(QA,0,0),(ATTEND,),(OUT,1,0),(OUT,0,1),(QB,0,1),(OUT,2,0),(OUT,1,1),(KV,1,0),(KV,0,1),(QB,1,0),(QA,1,0),(QA,0,1),(OUT,3,0),(OUT,2,1),(KV,2,0),(KV,1,1),(QB,1,1),
(QA,2,0),(OUT,3,1),(PROJECT,),(KV,3,0),(QB,2,0),(QA,1,1),(QA,3,0),(NORMALISE,),(KV,2,1),(KV,3,1),(FINISH,KV),(QB,2,1),(QA,2,1),(QA,3,1),(FINISH,QA),(QB,3,0),(QB,3,1),(FINISH,QB),]


def places(span_ref, rows):
    half = rows // 2
    row = lax.broadcasted_iota(jnp.int32, (rows, 1), 0)
    col = lax.broadcasted_iota(jnp.int32, (1, rows), 1)

    def position(device, offsets):
        first, second = span_ref[0, device], span_ref[1, device]
        return jnp.where(offsets < half, first * half + offsets, second * half + offsets - half)

    return row, col, position


def column(ref, h):
    return jnp.transpose(ref[0, h:h + 1, :])


def update(query, key, value, keep, m, l, acc):
    scores = lax.dot_general(
        query, key, (((1,), (1,)), ((), ())), preferred_element_type=jnp.float32
    ) * HEAD ** (-0.5)
    masked = jnp.where(keep, scores, -1e30)
    top = jnp.max(masked, axis=1, keepdims=True)
    m_new = top if m is None else jnp.maximum(m, top)
    p = jnp.where(keep, jnp.exp(scores - m_new), 0.0)
    l_new = jnp.sum(p, axis=1, keepdims=True)
    out = jnp.dot(p.astype(jnp.bfloat16), value, preferred_element_type=jnp.float32)
    if m is not None:
        decay = jnp.exp(m - m_new)
        l_new = l * decay + l_new
        out = acc * decay + out
    return m_new, l_new, out


def own_kernel(span_ref, in_buf, q_out, kv_out, max_out, sum_out, out_out):
    me = lax.axis_index("ctx")
    rows, unit = in_buf.shape[1:]
    row, col, position = places(span_ref, rows)
    keep = position(me, col) <= position(me, row)
    kv_out[0] = in_buf[0]
    for h in range(QHEADS):
        query = in_buf[1 + h // 2, :, (h % 2) * HEAD:(h % 2 + 1) * HEAD]
        m, l, acc = update(query, in_buf[0, :, :HEAD], in_buf[0, :, HEAD:], keep, None, None, None)
        q_out[0, :, h * HEAD:(h + 1) * HEAD] = query
        max_out[0, h:h + 1, :] = jnp.transpose(m)
        sum_out[0, h:h + 1, :] = jnp.transpose(l)
        out_out[0, :, h * HEAD:(h + 1) * HEAD] = acc


def kernel(
    sections,
    n,
    resid_hbm,
    queries_ref,
    keyvals_hbm,
    max_ref,
    sum_ref,
    run_ref,
    span_ref,
    gain_hbm,
    wq_hbm,
    wkv_hbm,
    wo_hbm,
    in_buf,
    wo_buf,
    w_buf,
    resid_buf,
    fin_buf,
    gain_buf,
    near_buf,
    att_buf,
    acc_buf,
    sq_buf,
    ship_buf,
    local_sem,
    send_sem,
    recv_sem,
    nsend_sem,
    nrecv_sem,
    xsend_sem,
    gain_sem,
    rsend_sem,
    rrecv_sem,
):
    sec = lax.axis_index("section")
    me = lax.axis_index("ctx")
    layers = n // 4
    z, y, c = me // 4, (me // 2) % 2, me % 2
    ahead = lax.rem(sec + 1, sections)
    behind = lax.rem(sec + sections - 1, sections)
    rows = resid_buf.shape[0]
    unit = w_buf.shape[-1]

    load_resid = pltpu.make_async_copy(resid_hbm.at[0], resid_buf, local_sem.at[0])
    load_out = pltpu.make_async_copy(wo_hbm.at[0], wo_buf.at[me], local_sem.at[1])
    load_out.start()
    load_resid.start()

    def index(zz, yy, cc):
        return zz * 4 + yy * 2 + cc

    barrier = pltpu.get_barrier_semaphore()
    fixed = [
        (sec, index(z, y, 1 - c)),
        (sec, index(z, 1 - y, c)),
        (sec, lax.rem(me + 1, n)),
        (sec, lax.rem(me + 2, n)),
        (sec, lax.rem(me + n - 1, n)),
        (sec, lax.rem(me + n - 2, n)),
        (ahead, me),
        (behind, me),
    ]
    for peer in fixed:
        pl.semaphore_signal(barrier, inc=1, device_id=peer, device_id_type=MESH)

    @pl.when(z > 0)
    def _():
        pl.semaphore_signal(barrier, inc=1, device_id=(sec, me - 4), device_id_type=MESH)

    @pl.when(z < layers - 1)
    def _():
        pl.semaphore_signal(barrier, inc=1, device_id=(sec, me + 4), device_id_type=MESH)

    ends = jnp.where(z > 0, 1, 0) + jnp.where(z < layers - 1, 1, 0)
    pl.semaphore_wait(barrier, len(fixed) + ends)

    def remote(src, dst, send, recv, device):
        return pltpu.make_async_remote_copy(
            src_ref=src, dst_ref=dst, send_sem=send, recv_sem=recv,
            device_id=device, device_id_type=MESH,
        )

    near_copy = remote(keyvals_hbm.at[0], near_buf.at[0], nsend_sem.at[0], nrecv_sem.at[0],
                       (sec, lax.rem(me + n - 1, n)))
    far_copy = remote(keyvals_hbm.at[0], near_buf.at[1], nsend_sem.at[1], nrecv_sem.at[1],
                      (sec, lax.rem(me + n - 2, n)))
    near_copy.start()
    far_copy.start()

    def slot(u, src):
        return wo_buf.at[src] if u == OUT else w_buf.at[u - 1, src]

    swaps = []
    for u, ref in ((KV, wkv_hbm.at[0]), (QA, wq_hbm.at[0, :, 0:unit]),
                   (QB, wq_hbm.at[0, :, unit:2 * unit])):
        swaps.append(remote(ref, slot(u, me), xsend_sem.at[u], recv_sem.at[u, me], (behind, me)))
    gain_copy = remote(gain_hbm, gain_buf, xsend_sem.at[0], gain_sem.at[0], (behind, me))
    swaps[2].start()
    swaps[0].start()
    gain_copy.start()
    swaps[1].start()

    def hop(u, src, way):
        target = {
            CORE: index(z, y, 1 - c), ACROSS: index(z, 1 - y, c), UP: me + 4, DOWN: me - 4,
        }[way]
        return remote(slot(u, src), slot(u, src), send_sem.at[way, u, src],
                      recv_sem.at[u, src], (sec, target))

    def arrive(u, src):
        hop(u, src, CORE).wait_recv()

    def each_hop(u, d, other, act, arrived=None):
        yy = 1 - y if other else y

        def go(src, ways):
            if arrived is not None:
                arrived(src)
            for way in ways:
                if way == UP:
                    @pl.when(z < layers - 1)
                    def _():
                        act(hop(u, src, UP))
                elif way == DOWN:
                    @pl.when(z > 0)
                    def _():
                        act(hop(u, src, DOWN))
                else:
                    act(hop(u, src, way))

        onward = u == ACROSS_FIRST or not other
        across = [ACROSS] if (not other and (u != ACROSS_FIRST or d == 0)) else []
        if d == 0:
            go(index(z, yy, c), ([UP, DOWN] if onward else []) + across + [CORE])
        else:
            @pl.when(z >= d)
            def _():
                go(index(z - d, yy, c), ([UP] if onward else []) + across + [CORE])

            @pl.when(z + d < layers)
            def _():
                go(index(z + d, yy, c), ([DOWN] if onward else []) + across + [CORE])

    def event(u, d, other):
        own = u == OUT and d == 0 and not other
        each_hop(u, d, other, lambda copy: copy.start(),
                 None if own else lambda src: arrive(u, src))

    load_out.wait()

    row, col, position = places(span_ref, rows)
    pos_mine = position(me, row)
    keep_far = position(lax.rem(me + 2, n), col) <= pos_mine
    keep_near = position(lax.rem(me + 1, n), col) <= pos_mine

    def attend(h):
        cols = slice(h * HEAD, (h + 1) * HEAD)
        query = queries_ref[0, :, cols]
        m, l, acc = column(max_ref, h), column(sum_ref, h), run_ref[0, :, cols]
        m, l, acc = update(query, near_buf[1, :, :HEAD], near_buf[1, :, HEAD:], keep_far, m, l, acc)
        m, l, acc = update(query, near_buf[0, :, :HEAD], near_buf[0, :, HEAD:], keep_near, m, l, acc)
        att_buf[:, cols] = (acc / l).astype(jnp.bfloat16)

    def project(step, carry):
        src = lax.rem(me + step, n)

        @pl.when(src % 2 != c)
        def _():
            arrive(OUT, src)

        at = pl.ds(pl.multiple_of(src * unit, unit), unit)
        block = jnp.dot(att_buf[...], wo_buf[src], preferred_element_type=jnp.float32)
        block = (resid_buf[:, at].astype(jnp.float32) + block).astype(jnp.bfloat16)
        fin_buf[src] = block
        wide = block.astype(jnp.float32)
        sq_buf[...] += wide * wide
        return carry

    def normalise(inverse, src, carry):
        at = pl.ds(pl.multiple_of(src * unit, unit), unit)
        wide = fin_buf[src].astype(jnp.float32)
        fin_buf[src] = (wide * inverse * gain_buf[:, at]).astype(jnp.bfloat16)
        return carry

    def finish(u):
        acc_buf[...] = jnp.zeros_like(acc_buf)

        def add(src, carry):
            @pl.when(src % 2 != c)
            def _():
                arrive(u, src)

            acc_buf[...] += jnp.dot(fin_buf[src], w_buf[u - 1, src], preferred_element_type=jnp.float32)
            return carry

        lax.fori_loop(0, n, add, 0)
        ship_buf[u - 1] = acc_buf[...].astype(jnp.bfloat16)
        copy = remote(ship_buf.at[u - 1], in_buf.at[u - 1], rsend_sem.at[u - 1],
                      rrecv_sem.at[u - 1], (ahead, me))
        copy.start()
        return copy

    results = []
    for step in ORDER:
        if step[0] < ATTEND:
            event(step[0], step[1], step[2] == 1)
        elif step[0] == ATTEND:
            far_copy.wait_recv()
            near_copy.wait_recv()
            for h in range(QHEADS):
                attend(h)
        elif step[0] == PROJECT:
            load_resid.wait()
            sq_buf[...] = jnp.zeros_like(sq_buf)
            lax.fori_loop(0, n, project, 0)
        elif step[0] == NORMALISE:
            gain_copy.wait_recv()
            mean_square = jnp.sum(sq_buf[...], axis=1, keepdims=True) * (1.0 / (n * unit))
            inverse = lax.rsqrt(mean_square + 1e-05)
            lax.fori_loop(0, n, functools.partial(normalise, inverse), 0)
        else:
            results.append(finish(step[1]))
    for copy in results:
        copy.wait_recv()

    near_copy.wait_send()
    far_copy.wait_send()
    gain_copy.wait_send()
    for copy in swaps + results:
        copy.wait_send()
    for u in (OUT, KV, QA, QB):
        for d in range(layers):
            for other in (False, True):
                each_hop(u, d, other, lambda copy: copy.wait_send())


def fused(mesh, *args):
    sections, n = mesh.shape["section"], mesh.shape["ctx"]
    resid, queries, keyvals, run_max, run_sum, run_out = args[:6]
    rows, width = resid.shape[1:]
    unit = keyvals.shape[2]
    bf16, f32 = jnp.bfloat16, jnp.float32
    vmem = pl.BlockSpec(memory_space=pltpu.VMEM)
    smem = pl.BlockSpec(memory_space=pltpu.SMEM)
    hbm = pl.BlockSpec(memory_space=pltpu.HBM)
    dma = pltpu.SemaphoreType.DMA
    turned_max, turned_sum = jnp.swapaxes(run_max, 1, 2), jnp.swapaxes(run_sum, 1, 2)
    turned_span = jnp.swapaxes(args[6], 0, 1)
    arrived = pl.pallas_call(
        functools.partial(kernel, sections, n),
        out_shape=jax.ShapeDtypeStruct((3, rows, unit), bf16),
        in_specs=[hbm, vmem, hbm, vmem, vmem, vmem, smem, hbm, hbm, hbm, hbm],
        out_specs=vmem,
        scratch_shapes=[
            pltpu.VMEM((n, 2 * unit, unit), bf16),
            pltpu.VMEM((3, n, unit, unit), bf16),
            pltpu.VMEM((rows, width), bf16),
            pltpu.VMEM((n, rows, unit), bf16),
            pltpu.VMEM((1, width), f32),
            pltpu.VMEM((2, rows, unit), bf16),
            pltpu.VMEM((rows, 2 * unit), bf16),
            pltpu.VMEM((rows, unit), f32),
            pltpu.VMEM((rows, unit), f32),
            pltpu.VMEM((3, rows, unit), bf16),
            dma((2,)),
            dma((4, 4, n)),
            dma((4, n)),
            dma((2,)),
            dma((2,)),
            dma((4,)),
            dma((1,)),
            dma((3,)),
            dma((3,)),
        ],
        compiler_params=pltpu.CompilerParams(
            collective_id=0, has_side_effects=True, vmem_limit_bytes=62 * 1024 * 1024
        ),
    )(resid, queries, keyvals, turned_max, turned_sum, run_out, turned_span, *args[7:])
    q_new, kv_new, max_new, sum_new, out_new = pl.pallas_call(
        own_kernel,
        out_shape=(
            jax.ShapeDtypeStruct(queries.shape, bf16),
            jax.ShapeDtypeStruct(keyvals.shape, bf16),
            jax.ShapeDtypeStruct(turned_max.shape, f32),
            jax.ShapeDtypeStruct(turned_sum.shape, f32),
            jax.ShapeDtypeStruct(run_out.shape, f32),
        ),
        in_specs=[smem, vmem],
        out_specs=[vmem] * 5,
    )(turned_span, arrived)
    return q_new, kv_new, jnp.swapaxes(max_new, 1, 2), jnp.swapaxes(sum_new, 1, 2), out_new


def passed_along(value, axis, steps):
    count = lax.axis_size(axis)
    pairs = [(source, (source + steps) % count) for source in range(count)]
    return lax.ppermute(value, axis, pairs)


def device_positions(span_pair, device, rows_here):
    half_rows = rows_here // 2
    span_row = lax.dynamic_slice_in_dim(span_pair, device, 1, 0)[0]
    offsets = jnp.arange(rows_here, dtype=jnp.int32)
    span_index = jnp.where(offsets < half_rows, span_row[0], span_row[1])
    return span_index * half_rows + offsets % half_rows


def flash_step(query_rows, key_block, pos_query, pos_key, old_max, old_sum, old_out):
    rows_here = query_rows.shape[0]
    query_heads = query_rows.reshape(rows_here, QHEADS, HEAD)
    key_part = key_block[:, :HEAD]
    value_part = key_block[:, HEAD:]
    scores = jnp.einsum(
        "qhd,kd->hqk", query_heads, key_part, preferred_element_type=jnp.float32
    ) * HEAD ** (-0.5)
    keep = pos_key[None, None, :] <= pos_query[None, :, None]
    masked = jnp.where(keep, scores, -1e30)
    prior_max = old_max.T
    new_max = jnp.maximum(prior_max, jnp.max(masked, axis=-1))
    exp_scores = jnp.where(keep, jnp.exp(scores - new_max[:, :, None]), 0.0)
    decay_factor = jnp.exp(prior_max - new_max)
    new_sum = old_sum.T * decay_factor + jnp.sum(exp_scores, axis=-1)
    rounded = exp_scores.astype(jnp.bfloat16)
    contrib = jnp.einsum("hqk,kd->qhd", rounded, value_part, preferred_element_type=jnp.float32)
    new_out = old_out.reshape(rows_here, QHEADS, HEAD) * decay_factor.T[:, :, None] + contrib
    return (new_max.T, new_sum.T, new_out.reshape(rows_here, QHEADS * HEAD))


def add_rows(normed, shard_rows):
    return jnp.dot(normed, shard_rows, preferred_element_type=jnp.float32)


def per_device(
    resid,
    queries,
    keyvals,
    run_max,
    run_sum,
    run_out,
    span_pair,
    norm_gain,
    w_query,
    w_keyval,
    w_out,
):
    cycle_size = lax.axis_size("ctx")
    my_index = lax.axis_index("ctx")
    rows_here = resid.shape[1]
    pos_mine = device_positions(span_pair, my_index, rows_here)
    pos_near = device_positions(span_pair, (my_index + 1) % cycle_size, rows_here)
    pos_far = device_positions(span_pair, (my_index + 2) % cycle_size, rows_here)
    keyval_own = keyvals[0]
    near_block = passed_along(keyval_own, "ctx", -1)
    far_block = passed_along(near_block, "ctx", -1)
    max_now, sum_now, out_now = flash_step(
        queries[0], far_block, pos_mine, pos_far, run_max[0], run_sum[0], run_out[0]
    )
    max_now, sum_now, out_now = flash_step(
        queries[0], near_block, pos_mine, pos_near, max_now, sum_now, out_now
    )
    divided = out_now.reshape(rows_here, QHEADS, HEAD) / sum_now[:, :, None]
    attended = divided.reshape(rows_here, QHEADS * HEAD).astype(jnp.bfloat16)
    projected = jnp.dot(
        attended,
        lax.all_gather(w_out[0], "ctx", axis=1, tiled=True),
        preferred_element_type=jnp.float32,
    )
    finished = (resid[0].astype(jnp.float32) + projected).astype(jnp.bfloat16)
    incoming = passed_along(finished, "section", 1)
    wide = incoming.astype(jnp.float32)
    mean_square = jnp.mean(wide * wide, axis=-1, keepdims=True)
    normed = (wide * lax.rsqrt(mean_square + 1e-05) * norm_gain[0][None, :]).astype(jnp.bfloat16)

    def add_one(shard_rows):
        return add_rows(normed, shard_rows)

    query_sum = add_one(lax.all_gather(w_query[0], "ctx", axis=0, tiled=True))
    keyval_sum = add_one(lax.all_gather(w_keyval[0], "ctx", axis=0, tiled=True))
    query_new = query_sum.astype(jnp.bfloat16)
    keyval_new = keyval_sum.astype(jnp.bfloat16)
    start_max = jnp.full((rows_here, QHEADS), -1e30, jnp.float32)
    start_sum = jnp.zeros((rows_here, QHEADS), jnp.float32)
    start_out = jnp.zeros((rows_here, QHEADS * HEAD), jnp.float32)
    max_new, sum_new, out_new = flash_step(
        query_new, keyval_new, pos_mine, pos_mine, start_max, start_sum, start_out
    )
    return (query_new[None], keyval_new[None], max_new[None], sum_new[None], out_new[None])


def solution(mesh):
    placed = (
        P("section", "ctx", None),
        P("section", "ctx", None),
        P("section", "ctx", None),
        P("section", "ctx", None),
        P("section", "ctx", None),
        P("section", "ctx", None),
        P(),
        P("section", None),
        P("section", "ctx", None),
        P("section", "ctx", None),
        P("section", None, "ctx"),
    )
    def local(*args):
        rows, width = args[0].shape[1:]
        unit = args[2].shape[2]
        n = mesh.shape["ctx"]
        even = n % 4 == 0 and n <= 16 and mesh.shape["section"] > 1
        if even and rows == unit == 2 * HEAD and width == n * unit and rows % 32 == 0:
            return fused(mesh, *args)
        return per_device(*args)

    return jax.shard_map(
        local,
        mesh=mesh,
        in_specs=placed,
        out_specs=(
            P("section", "ctx", None),
            P("section", "ctx", None),
            P("section", "ctx", None),
            P("section", "ctx", None),
            P("section", "ctx", None),
        ),
        check_vma=False,
    )
```
